256 devices in a mesh: frame: 16 (over x, z_hi), row: 8 (over y, core), head: 2 (over z_lo).
Axes of the slice: x: 4, y: 4, z: 8 (z_hi: 4, z_lo: 2; z = z_hi * 2 + z_lo), core: 2. Of those that a mesh axis runs over, the one named last changes fastest.
Arguments:
- queries: bfloat16 [32, 16, 32, 3072], P('frame', 'row', 'head'), may hold values from -6 to 6
- key_tokens: bfloat16 [32, 16, 32, 3072], P('frame', 'row', 'head'), may hold values from -6 to 6
- values: bfloat16 [32, 16, 32, 3072], P('frame', 'row', 'head'), may hold values from -6 to 6
- outputs: bfloat16 [32, 16, 32, 3072], P('frame', 'row', 'head'), may hold values from -6 to 6
- grad_out: bfloat16 [32, 16, 32, 3072], P('frame', 'row', 'head'), may hold values from -48 to 48
- log_sums: float32 [24, 32, 16, 32], P('head', 'frame', 'row'), may hold values from 5.5 to 7.5
Outputs:
- grad_queries: bfloat16 [32, 16, 32, 3072], P('frame', 'row', 'head')
- grad_keys: bfloat16 [32, 16, 32, 3072], P('frame', 'row', 'head')
- grad_values: bfloat16 [32, 16, 32, 3072], P('frame', 'row', 'head')
The draws below stay inside these ranges and needn't reach their ends.
All inputs are finite; a program needn't handle non-finite values.
Results may differ from the reference program's by a relative error of at most 0.0055.
Values may be sent and summed in bfloat16 or wider, within the bound.
No kernel may reach another device: no remote copies, remote signals or barrier semaphores. Data moves between devices by JAX's collectives and lax.ppermute only.
A program may use at most 128 MiB of HBM per device.

```python
import math
import jax
import jax.numpy as jnp
from jax import lax

C = 32
HD = 128
HEADS = 24
FRAMES = 32
ROWS = 16


def level_of(stream_key, shape, split, smallest, top_value):
    factor_of = 1.0
    for dim, blocks in split:
        steps = jax.random.uniform(jax.random.fold_in(jax.random.fold_in(stream_key, 6), dim), (blocks,), jnp.float32, smallest / len(split), top_value / len(split))
        factor_of = factor_of * jnp.repeat(jnp.exp(steps), shape[dim] // blocks).reshape((-1,) + (1,) * (len(shape) - 1 - dim))
    return factor_of


def noise(own_key, extent, scale, most, pieces=(), dtype=jnp.bfloat16):
    values = jax.random.normal(own_key, extent, jnp.float32) * scale
    if len(pieces) > 0:
        values = level_of(own_key, extent, pieces, -0.22, 0.18) * values
    return jnp.clip(values, min=-most, max=most).astype(dtype)


def setup_inputs(seed: int = 0) -> dict:
    seeds = jax.random.split(jax.random.key(seed), 7)
    return {
        "queries": noise(seeds[0], (FRAMES, ROWS, C, HEADS * HD), 1.0, 6.0, ((0, 16), (1, 8), (2, 2))),
        "key_tokens": noise(seeds[1], (FRAMES, ROWS, C, HEADS * HD), 1.0, 6.0, ((0, 16), (1, 8), (2, 2))),
        "values": noise(seeds[2], (FRAMES, ROWS, C, HEADS * HD), 1.0, 6.0, ((0, 16), (1, 8), (2, 2))),
        "outputs": noise(seeds[3], (FRAMES, ROWS, C, HEADS * HD), 1.0, 6.0, ((0, 16), (1, 8), (2, 2))),
        "grad_out": noise(seeds[4], (FRAMES, ROWS, C, HEADS * HD), 8.0, 48.0, ((0, 16), (1, 8), (2, 2))),
        "log_sums": jnp.clip(5.5 + 2.0 * jax.random.uniform(seeds[5], (HEADS, FRAMES, ROWS, C), jnp.float32) ** level_of(seeds[5], (HEADS, FRAMES, ROWS, C), ((0, 2), (1, 16), (2, 8)), -0.2, 0.2), 5.5, 7.5),
    }


def head_grads(query_head, key_head, value_head, output_head, grad_head, log_sum):
    frame_total = query_head.shape[0]
    row_total = query_head.shape[1]
    scaling = 1.0 / math.sqrt(HD)
    query_full = query_head.astype(jnp.float32)
    grad_full = grad_head.astype(jnp.float32)
    grad_dot = lax.optimization_barrier(jnp.sum(grad_full * output_head.astype(jnp.float32), axis=-1))
    key_padded = jnp.pad(key_head.astype(jnp.float32), ((2, 2), (2, 2), (0, 0), (0, 0)))
    value_padded = jnp.pad(value_head.astype(jnp.float32), ((2, 2), (2, 2), (0, 0), (0, 0)))
    frame_index = jnp.arange(frame_total)
    row_index = jnp.arange(row_total)
    grad_query = jnp.zeros(query_head.shape, jnp.float32)
    grad_key_pad = jnp.zeros(key_padded.shape, jnp.float32)
    grad_value_pad = jnp.zeros(key_padded.shape, jnp.float32)
    for frame_step in range(5):
        frame_valid = (frame_index + frame_step - 2 >= 0) & (frame_index + frame_step - 2 < frame_total)
        for row_step in range(5):
            row_valid = (row_index + row_step - 2 >= 0) & (row_index + row_step - 2 < row_total)
            valid_keys = frame_valid[:, None, None, None] & row_valid[None, :, None, None]
            far_key = key_padded[frame_step:frame_step + frame_total, row_step:row_step + row_total]
            far_value = value_padded[frame_step:frame_step + frame_total, row_step:row_step + row_total]
            scores = jnp.einsum('frcd,frxd->frcx', query_full, far_key) * scaling
            prob_full = jnp.where(valid_keys, jnp.exp(scores - log_sum[..., None]), 0.0)
            prob_half = lax.optimization_barrier(prob_full.astype(jnp.bfloat16)).astype(jnp.float32)
            grad_prob = jnp.einsum('frcd,frxd->frcx', grad_full, far_value)
            grad_score = lax.optimization_barrier((prob_full * (grad_prob - grad_dot[..., None])).astype(jnp.bfloat16)).astype(jnp.float32)
            grad_query = grad_query + jnp.einsum('frcx,frxd->frcd', grad_score, far_key) * scaling
            grad_key_pad = grad_key_pad.at[frame_step:frame_step + frame_total, row_step:row_step + row_total].add(jnp.einsum('frcx,frcd->frxd', grad_score, query_full) * scaling)
            grad_value_pad = grad_value_pad.at[frame_step:frame_step + frame_total, row_step:row_step + row_total].add(jnp.einsum('frcx,frcd->frxd', prob_half, grad_full))
    return (grad_query.astype(jnp.bfloat16), grad_key_pad[2:-2, 2:-2].astype(jnp.bfloat16), grad_value_pad[2:-2, 2:-2].astype(jnp.bfloat16))

def split_heads(tokens):
    shaped = tokens.reshape(tokens.shape[0], tokens.shape[1], tokens.shape[2], HEADS, HD)
    return jnp.moveaxis(shaped, 3, 0)

def merge_heads(grads):
    moved = jnp.moveaxis(grads, 0, 3)
    return moved.reshape(moved.shape[0], moved.shape[1], moved.shape[2], HEADS * HD)

def reference(queries, key_tokens, values, outputs, grad_out, log_sums):
    bundle = (split_heads(queries), split_heads(key_tokens), split_heads(values), split_heads(outputs), split_heads(grad_out), log_sums)
    per_head = lax.map(lambda parts: head_grads(*parts), bundle)
    return (merge_heads(per_head[0]), merge_heads(per_head[1]), merge_heads(per_head[2]))
```

```python
import math

import jax
import jax.numpy as jnp
from jax import lax
from jax.experimental import pallas as pl
from jax.experimental.pallas import tpu as pltpu
from jax.sharding import Mesh
from jax.sharding import PartitionSpec as P

HD = 128
HEADS = 24
F, R, CH, C = 2, 2, 16, 32
ZH, ZL = 4, 2
Z = ZH * ZL
HL = HEADS // Z
FX = F * ZH
FE = FX + 4
NX, NROW = 4, 8
RING = ("zh", "zl")
BIG = -float(2**30)
SCALE = 1.0 / math.sqrt(HD)
LOG2E = math.log2(math.e)
DOT0, LSE0, LSE1, FR0, RW0 = 0, 16, 80, 32, 48
VMEM = 56 * 1024 * 1024
BF, F32 = jnp.bfloat16, jnp.float32


def params(**kw):
    return pltpu.CompilerParams(vmem_limit_bytes=VMEM, **kw)


def call(kernel, outs, n_in, name, flops=0, nbytes=1 << 20, scratch=()):
    whole = pl.BlockSpec(memory_space=pltpu.VMEM)
    return pl.pallas_call(
        kernel,
        out_shape=outs,
        in_specs=[whole] * n_in,
        out_specs=jax.tree.map(lambda _: whole, outs),
        scratch_shapes=list(scratch),
        compiler_params=params(),
        cost_estimate=pl.CostEstimate(flops=flops, bytes_accessed=nbytes, transcendentals=0),
        name=name,
    )


def shape(*dims, dtype=BF):
    return jax.ShapeDtypeStruct(dims, dtype)


def lanes(*dims):
    return lax.broadcasted_iota(jnp.int32, dims, len(dims) - 1)


def three(x):
    hi = x.astype(BF).astype(F32)
    mid = (x - hi).astype(BF).astype(F32)
    lo = (x - hi - mid).astype(BF).astype(F32)
    return hi, mid, lo


def head_of(dest, h):
    return (HEADS // ZL) * (dest % ZL) + HL * (dest // ZL) + h


def pack_q(q_ref, do_ref, o_ref, lse_ref, out_ref):
    parts = three(lse_ref[...] * math.sqrt(HD))
    row = lax.broadcasted_iota(jnp.int32, (128, 16), 0)
    col = lax.broadcasted_iota(jnp.int32, (128, 16), 1)
    spread = jnp.zeros((128, 128), F32)
    for p, part in enumerate(parts):
        put = jnp.zeros((128, 16), F32)
        for h in range(HL):
            put = jnp.where((row % 16 == 3 * h + p) & (row < 64) & (col == (row // 16) * HL + h), 1.0, put)
        spread = spread + jnp.dot(put.astype(BF), part.astype(BF), preferred_element_type=F32)
    turned = spread.T.reshape(F * R, ZL, CH, 128)
    both = turned[:, 0] + pltpu.roll(turned[:, 1].reshape(F * R * CH, 128), 64, 1).reshape(F * R, CH, 128)
    both = both.reshape(F * R * CH, 128)
    lane = lanes(F * R * CH, 128)
    for dest in range(Z):
        side = jnp.zeros((F * R * CH, 128), F32)
        for h in range(HL):
            at = head_of(dest, h) * HD
            q = q_ref[:, :, :, at : at + HD]
            g = do_ref[:, :, :, at : at + HD]
            out_ref[dest, h] = q
            out_ref[dest, HL + h] = g
            o = o_ref[:, :, :, at : at + HD]
            dot = jnp.sum((g.astype(F32) * o.astype(F32)).reshape(F * R * CH, HD), axis=-1, keepdims=True)
            for p, part in enumerate(three(dot)):
                side = jnp.where(lane == DOT0 + 3 * h + p, part, side)
        zh = dest // ZL
        turn = (LSE0 - 16 * zh) % 128
        lse = both if turn == 0 else pltpu.roll(both, turn, 1)
        keep = ((lane >= LSE0) & (lane < LSE0 + 9)) | ((lane >= LSE1) & (lane < LSE1 + 9))
        side = jnp.where(keep, lse, side)
        out_ref[dest, 2 * HL] = side.astype(BF).reshape(F, R, CH, 128)


def pack_kv(k_ref, v_ref, out_ref):
    for dest in range(Z):
        for h in range(HL):
            at = head_of(dest, h) * HD
            out_ref[dest, h] = k_ref[:, :, :, at : at + HD]
            out_ref[dest, HL + h] = v_ref[:, :, :, at : at + HD]


def place(blocks, in_ref, ext_ref, lo_ref, hi_ref):
    for src in range(Z):
        zh, zl = src // ZL, src % ZL
        cols = slice(zl * CH, zl * CH + CH)
        for b in range(blocks):
            for f in range(F):
                piece = in_ref[src, b, f]
                ext_ref[2 + F * zh + f, b, :, cols] = piece
                if zh == 0:
                    lo_ref[f, b, :, cols] = piece
                if zh == ZH - 1:
                    hi_ref[f, b, :, cols] = piece


def gather_q(in_ref, ext_ref, lo_ref, hi_ref):
    place(2 * HL, in_ref, ext_ref, lo_ref, hi_ref)
    mine = lax.axis_index("zl")
    n = F * R * CH
    lane = lanes(n, 128)
    for src in range(Z):
        zh, zl = src // ZL, src % ZL
        cols = slice(zl * CH, zl * CH + CH)
        dot = in_ref[src, 2 * HL].astype(F32).reshape(n, 128)
        lse = in_ref[ZL * zh + mine, 2 * HL].astype(F32).reshape(n, 128)
        if zl == 1:
            lse = pltpu.roll(lse, 64, 1)
        side = jnp.where(lane < 16, dot, jnp.where(lane < 32, lse, 0.0))
        side = side.astype(BF).reshape(F, R, CH, 128)
        for f in range(F):
            ext_ref[2 + F * zh + f, 2 * HL, :, cols] = side[f]
            if zh == 0:
                lo_ref[f, 2 * HL, :, cols] = side[f]
            if zh == ZH - 1:
                hi_ref[f, 2 * HL, :, cols] = side[f]


def gather_kv(in_ref, ext_ref, lo_ref, hi_ref):
    place(2 * HL, in_ref, ext_ref, lo_ref, hi_ref)


def fill_x(ext_ref, before_ref, after_ref, out_ref, sem):
    del ext_ref
    one = pltpu.make_async_copy(before_ref, out_ref.at[pl.ds(0, 2)], sem.at[0])
    two = pltpu.make_async_copy(after_ref, out_ref.at[pl.ds(FE - 2, 2)], sem.at[1])
    one.start()
    two.start()
    one.wait()
    two.wait()


def own_marks(group):
    dims = (F * R * C, 128)
    token = lax.broadcasted_iota(jnp.int32, dims, 0)
    lane = lanes(*dims)
    frame = 2 + F * group + token // (R * C)
    row = 2 + (token // C) % R
    x, r = lax.axis_index("x"), lax.axis_index("row")
    e = lane - FR0
    real = x * FX + e - 2
    bad = (jnp.abs(e - frame) > 2) | (real < 0) | (real >= NX * FX)
    out = jnp.where((e >= 0) & (e < FE) & bad, BIG, 0.0)
    e = lane - RW0
    real = r * R + e - 2
    bad = (jnp.abs(e - row) > 2) | (real < 0) | (real >= NROW * R)
    return jnp.where((e >= 0) & (e < R + 4) & bad, BIG, out)


def far_marks(part):
    dims = (FE, R * C, 128)
    lane = lanes(*dims)
    frame = lax.broadcasted_iota(jnp.int32, dims, 0)
    row = R * part + lax.broadcasted_iota(jnp.int32, dims, 1) // C
    return jnp.where((lane == FR0 + frame) | (lane == RW0 + row), 1.0, 0.0)


def minus_at(start, n):
    lane = lanes(n, 128)
    return jnp.where((lane >= start) & (lane < start + 3), -1.0, 0.0)


def nt(a, b):
    return lax.dot_general(a, b, (((1,), (1,)), ((), ())), preferred_element_type=F32)


def key_grads(qm_ref, qo_ref, qp_ref, kv_ref, out_ref, side_ref):
    n = F * R * C
    refs = (qm_ref, qo_ref, qp_ref)
    lane = lanes(FE, R * C, 128)
    for part, ref in enumerate(refs):
        data = ref[:, 2 * HL].astype(F32).reshape(FE, R * C, 128)
        side_ref[part] = jnp.where(lane < 32, data, far_marks(part)).astype(BF)
    for group in range(ZH):
        marks = own_marks(group)
        frames = slice(F * group, F * group + F + 4)
        m = (F + 4) * R * C
        side = jnp.concatenate([side_ref[part, frames].reshape(m, 128) for part in range(3)], axis=0)
        for h in range(HL):
            own = slice(2 + F * group, 2 + F * group + F)
            k = kv_ref[own, h].reshape(n, HD)
            v = kv_ref[own, HL + h].reshape(n, HD)
            q = jnp.concatenate([ref[frames, h].reshape(m, HD) for ref in refs], axis=0)
            g = jnp.concatenate([ref[frames, HL + h].reshape(m, HD) for ref in refs], axis=0)
            k_side = (marks + minus_at(LSE0 + 3 * h, n)).astype(BF)
            v_side = minus_at(DOT0 + 3 * h, n).astype(BF)
            s = nt(jnp.concatenate([k, k_side], axis=1), jnp.concatenate([q, side], axis=1))
            d = nt(jnp.concatenate([v, v_side], axis=1), jnp.concatenate([g, side], axis=1))
            prob = jnp.exp2(s * (SCALE * LOG2E))
            score = (prob * d).astype(BF)
            dv = jnp.dot(prob.astype(BF), g, preferred_element_type=F32)
            dk = jnp.dot(score, q, preferred_element_type=F32) * SCALE
            dk = dk.astype(BF).reshape(F, R, C, HD)
            dv = dv.astype(BF).reshape(F, R, C, HD)
            for zl in range(ZL):
                cols = slice(zl * CH, zl * CH + CH)
                out_ref[ZL * group + zl, h] = dk[:, :, cols]
                out_ref[ZL * group + zl, HL + h] = dv[:, :, cols]


def query_grads(km_ref, ko_ref, kp_ref, q_ref, out_ref):
    n = F * R * C
    refs = (km_ref, ko_ref, kp_ref)
    lane = lanes(n, 128)
    for group in range(ZH):
        frames = slice(F * group, F * group + F + 4)
        own = slice(2 + F * group, 2 + F * group + F)
        m = (F + 4) * R * C
        data = q_ref[own, 2 * HL].astype(F32).reshape(n, 128)
        side = jnp.where(lane < 32, data, own_marks(group)).astype(BF)
        far = jnp.concatenate([far_marks(part)[frames].reshape(m, 128) for part in range(3)], axis=0)
        for h in range(HL):
            q = q_ref[own, h].reshape(n, HD)
            g = q_ref[own, HL + h].reshape(n, HD)
            k = jnp.concatenate([ref[frames, h].reshape(m, HD) for ref in refs], axis=0)
            v = jnp.concatenate([ref[frames, HL + h].reshape(m, HD) for ref in refs], axis=0)
            k_side = (far + minus_at(LSE0 + 3 * h, 3 * m)).astype(BF)
            v_side = minus_at(DOT0 + 3 * h, 3 * m).astype(BF)
            s = nt(jnp.concatenate([q, side], axis=1), jnp.concatenate([k, k_side], axis=1))
            d = nt(jnp.concatenate([g, side], axis=1), jnp.concatenate([v, v_side], axis=1))
            score = (jnp.exp2(s * (SCALE * LOG2E)) * d).astype(BF)
            dq = jnp.dot(score, k, preferred_element_type=F32) * SCALE
            dq = dq.astype(BF).reshape(F, R, C, HD)
            for zl in range(ZL):
                out_ref[ZL * group + zl, h] = dq[:, :, zl * CH : zl * CH + CH]


def unpack(in_ref, *out_refs):
    for i, out_ref in enumerate(out_refs):
        for src in range(Z):
            for h in range(HL):
                at = head_of(src, h) * HD
                out_ref[:, :, :, at : at + HD] = in_ref[src, HL * i + h]


def exchange(sends):
    return lax.all_to_all(sends, RING, split_axis=0, concat_axis=0, tiled=True)


def shift(block, axis, by):
    count = NX if axis == "x" else NROW
    return lax.ppermute(block, axis, [(i, (i + by) % count) for i in range(count)])


def with_x(ext, lo, hi):
    before = shift(hi, "x", 1)
    after = shift(lo, "x", -1)
    anywhere = pl.BlockSpec(memory_space=pl.ANY)
    return pl.pallas_call(
        fill_x,
        out_shape=shape(*ext.shape),
        in_specs=[anywhere] * 3,
        out_specs=anywhere,
        scratch_shapes=[pltpu.SemaphoreType.DMA((2,))],
        input_output_aliases={0: 0},
        compiler_params=params(),
        name="fill_x",
    )(ext, before, after)


def gathered(kernel, blocks, arrived, name):
    outs = (
        shape(FE, blocks, R, C, HD),
        shape(F, blocks, R, C, HD),
        shape(F, blocks, R, C, HD),
    )
    return call(kernel, outs, 1, name)(arrived)


def body(queries, key_tokens, values, outputs, grad_out, log_sums):
    lse = jnp.pad(log_sums.reshape(HEADS // ZL, F * R * C), ((0, 4), (0, 0)))
    sent_q = call(pack_q, shape(Z, 2 * HL + 1, F, R, CH, HD), 4, "pack_q")(queries, grad_out, outputs, lse)
    sent_kv = call(pack_kv, shape(Z, 2 * HL, F, R, CH, HD), 2, "pack_kv")(key_tokens, values)
    q_here = exchange(sent_q)
    kv_here = exchange(sent_kv)
    q_ext = with_x(*gathered(gather_q, 2 * HL + 1, q_here, "gather_q"))
    q_before, q_after = shift(q_ext, "row", 1), shift(q_ext, "row", -1)
    kv_own, kv_lo, kv_hi = gathered(gather_kv, 2 * HL, kv_here, "gather_kv")
    kv_ext = with_x(kv_own, kv_lo, kv_hi)
    kv_before, kv_after = shift(kv_ext, "row", 1), shift(kv_ext, "row", -1)
    pairs = ZH * HL * F * R * C * (F + 4) * 3 * R * C
    grads_kv = call(
        key_grads,
        shape(Z, 2 * HL, F, R, CH, HD),
        4,
        "key_grads",
        flops=pairs * 1536,
        scratch=[pltpu.VMEM((3, FE, R * C, 128), BF)],
    )(q_before, q_ext, q_after, kv_ext)
    kv_back = exchange(grads_kv)
    grads_q = call(query_grads, shape(Z, HL, F, R, CH, HD), 4, "query_grads", flops=pairs * 1280)(
        kv_before, kv_ext, kv_after, q_ext
    )
    q_back = exchange(grads_q)
    block = shape(F, R, CH, HEADS * HD)
    key_out, value_out = call(unpack, (block, block), 1, "unpack_kv")(kv_back)
    (query_out,) = call(unpack, (block,), 1, "unpack_q")(q_back)
    return query_out, key_out, value_out


def solution(mesh):
    fine = Mesh(mesh.devices.reshape(NX, ZH, NROW, ZL), ("x", "zh", "row", "zl"))
    block = P(("x", "zh"), "row", "zl", None)
    return jax.shard_map(
        body,
        mesh=fine,
        in_specs=(block,) * 5 + (P("zl", ("x", "zh"), "row", None),),
        out_specs=(block,) * 3,
        check_vma=False,
    )
```

```python
import math

import jax
import jax.numpy as jnp
from jax import lax
from jax.experimental import pallas as pl
from jax.experimental.pallas import tpu as pltpu
from jax.sharding import Mesh
from jax.sharding import PartitionSpec as P

HD = 128
HEADS = 24
F, R, CH = 2, 2, 16
ZH, ZL = 4, 2
Z = ZH * ZL
N = F * R * CH
HL = HEADS // Z
FX = F * ZH
FE = FX + 4
NX, NROW = 4, 8
RING = ("zh", "zl")
FAR = (4, 3, 5, 2, 6, 1, 7)
BIG = -float(2**30)
SCALE = 1.0 / math.sqrt(HD)
LOG2E = math.log2(math.e)
DOT0, LSE0, LSE1, FR0, RW0 = 0, 16, 80, 32, 48
VMEM = 28 * 1024 * 1024
SPAN = 2
BF, F32 = jnp.bfloat16, jnp.float32


def params(**kw):
    return pltpu.CompilerParams(vmem_limit_bytes=VMEM, **kw)


def call(kernel, outs, n_in, name, flops=0, nbytes=1 << 20, scratch=(), where=pltpu.VMEM, after=()):
    whole = pl.BlockSpec(memory_space=where)
    inner = lambda *refs: kernel(*refs[:n_in], *refs[n_in + len(after) :])
    made = pl.pallas_call(
        inner,
        out_shape=outs,
        in_specs=[whole] * n_in + [pl.BlockSpec(memory_space=pl.ANY)] * len(after),
        out_specs=jax.tree.map(lambda _: pl.BlockSpec(memory_space=pltpu.VMEM), outs),
        scratch_shapes=list(scratch),
        compiler_params=params(),
        cost_estimate=pl.CostEstimate(flops=flops, bytes_accessed=nbytes, transcendentals=0),
        name=name,
    )
    return lambda *args: made(*args, *after)


def shape(*dims, dtype=BF):
    return jax.ShapeDtypeStruct(dims, dtype)


def lanes(*dims):
    return lax.broadcasted_iota(jnp.int32, dims, len(dims) - 1)


def three(x):
    hi = x.astype(BF).astype(F32)
    mid = (x - hi).astype(BF).astype(F32)
    lo = (x - hi - mid).astype(BF).astype(F32)
    return hi, mid, lo


def head_of(dest, h):
    return (HEADS // ZL) * (dest % ZL) + HL * (dest // ZL) + h


def ring_place():
    return lax.axis_index("zh") * ZL + lax.axis_index("zl")


def head_lanes(dest, h):
    return pl.ds(pl.multiple_of(head_of(dest, h) * HD, HD), HD)


def pack(q_ref, do_ref, o_ref, k_ref, v_ref, lse_ref, *out_refs):
    parts = three(lse_ref[...] * math.sqrt(HD))
    row = lax.broadcasted_iota(jnp.int32, (128, 16), 0)
    col = lax.broadcasted_iota(jnp.int32, (128, 16), 1)
    spread = jnp.zeros((128, 128), F32)
    for p, part in enumerate(parts):
        put = jnp.zeros((128, 16), F32)
        for h in range(HL):
            put = jnp.where((row % 16 == 3 * h + p) & (row < 64) & (col == (row // 16) * HL + h), 1.0, put)
        spread = spread + jnp.dot(put.astype(BF), part.astype(BF), preferred_element_type=F32)
    turned = spread.T.reshape(F * R, ZL, CH, 128)
    second = pltpu.roll(turned[:, 1].reshape(N, 128), 64, 1)
    both = turned[:, 0].reshape(N, 128) + second
    lane = lanes(N, 128)
    keep = ((lane >= LSE0) & (lane < LSE0 + 9)) | ((lane >= LSE1) & (lane < LSE1 + 9))
    for k, out_ref in enumerate(out_refs):
        dest = lax.rem(ring_place() + k, Z)
        side = jnp.zeros((N, 128), F32)
        for h in range(HL):
            at = head_lanes(dest, h)
            g = do_ref[:, :, :, at]
            out_ref[2 * h] = q_ref[:, :, :, at]
            out_ref[2 * h + 1] = g
            out_ref[2 * HL + 1 + 2 * h] = k_ref[:, :, :, at]
            out_ref[2 * HL + 2 + 2 * h] = v_ref[:, :, :, at]
            dot = jnp.sum((g.astype(F32) * o_ref[:, :, :, at].astype(F32)).reshape(N, HD), axis=-1, keepdims=True)
            for p, part in enumerate(three(dot)):
                side = jnp.where(lane == DOT0 + 3 * h + p, part, side)
        lse = pltpu.roll(both, lax.rem(128 + LSE0 - 16 * (dest // ZL), 128), 1)
        out_ref[2 * HL] = jnp.where(keep, lse, side).astype(BF).reshape(F, R, CH, 128)


def gather_q(*refs):
    in_refs, (out_ref, lo_ref, hi_ref) = refs[:Z], refs[Z:]
    for k, in_ref in enumerate(in_refs):
        out_ref[lax.rem(ring_place() + Z - k, Z)] = in_ref[: 2 * HL + 1]
    mine = lax.axis_index("zl")
    lane = lanes(N, 128)
    for zh in range(ZH):
        lse = out_ref[ZL * zh + mine, 2 * HL].astype(F32).reshape(N, 128)
        for zl in range(ZL):
            dot = out_ref[ZL * zh + zl, 2 * HL].astype(F32).reshape(N, 128)
            here = lse if zl == 0 else pltpu.roll(lse, 64, 1)
            side = jnp.where(lane < 16, dot, jnp.where(lane < 32, here, 0.0))
            out_ref[ZL * zh + zl, 2 * HL] = side.astype(BF).reshape(F, R, CH, 128)
    lo_ref[...] = out_ref[:ZL]
    hi_ref[...] = out_ref[Z - ZL :]


def gather_kv(*refs):
    in_refs, (out_ref, lo_ref, hi_ref) = refs[:Z], refs[Z:]
    for k, in_ref in enumerate(in_refs):
        out_ref[lax.rem(ring_place() + Z - k, Z)] = in_ref[2 * HL + 1 :]
    lo_ref[...] = out_ref[:ZL]
    hi_ref[...] = out_ref[Z - ZL :]


def bad_frames(e, frame):
    real = lax.axis_index("x") * FX + e - 2
    return (jnp.abs(e - frame) > 2) | (real < 0) | (real >= NX * FX)


def bad_rows(e, row):
    real = lax.axis_index("row") * R + e - 2
    return (jnp.abs(e - row) > 2) | (real < 0) | (real >= NROW * R)


def far_place(part, group, dims, axis):
    token = lax.broadcasted_iota(jnp.int32, dims, axis)
    frame = F * (group + token // (ZL * N)) + (token // (R * CH)) % F
    return frame, R * part + (token // CH) % R


def seen(own, sides, group, block):
    first, last = group - 1, group + SPAN + 1
    pieces = [own[ZL * max(first, 0) : ZL * min(last, ZH), block]]
    if first < 0:
        pieces.insert(0, sides[:ZL, block])
    if last > ZH:
        pieces.append(sides[ZL:, block])
    pieces = [piece.reshape(-1, 128) for piece in pieces]
    return pieces[0] if len(pieces) == 1 else jnp.concatenate(pieces, axis=0)


def by_class(rows):
    m = rows.shape[1]
    spread = [jnp.broadcast_to(rows[i : i + 1], (CH, m)) for i in range(SPAN * F * R)]
    order = [z * F * R + i for z in range(SPAN) for _ in range(ZL) for i in range(F * R)]
    return jnp.concatenate([spread[i] for i in order], axis=0)


def nt(a, b):
    return lax.dot_general(a, b, (((1,), (1,)), ((), ())), preferred_element_type=F32)


def fetch(in_refs, bufs, sems):
    copies = {}
    for h in [HL] + list(range(HL)):
        for i, (ref, buf) in enumerate(zip(in_refs, bufs)):
            size = 2 if h < HL else 1
            if 2 * h < buf.shape[1]:
                at = pl.ds(2 * h, size)
                copies[h, i] = pltpu.make_async_copy(ref.at[:, at], buf.at[:, at], sems.at[h, i])
                copies[h, i].start()

    def ready(h):
        for (at, _), copy in copies.items():
            if at == h:
                copy.wait()

    return ready


def key_grads(*refs):
    in_refs, out_ref, bufs, sems = refs[:7], refs[7], refs[8:15], refs[15]
    ready = fetch(in_refs, bufs, sems)
    parts, kv = list(zip(bufs[:3], bufs[3:6])), bufs[6]
    n, m = SPAN * ZL * N, (SPAN + 2) * ZL * N
    lane = lanes(m, 128)
    ready(HL)
    shifts = {}
    for group in range(0, ZH, SPAN):
        dims = (32, 128)
        row = lax.broadcasted_iota(jnp.int32, dims, 0)
        pick = lanes(*dims)
        e = pick - FR0
        bad = bad_frames(e, 2 + F * group + (row % 8) // R) & (e >= 0) & (e < FE)
        marks = jnp.where(bad, BIG, 0.0)
        e = pick - RW0
        bad = bad_rows(e, 2 + row % R) & (e >= 0) & (e < R + 4)
        marks = jnp.where(bad, BIG, marks)
        at = pick - LSE0 - 3 * (row // 8)
        marks = jnp.where((at >= 0) & (at < 3), -1.0, marks)
        at = pick - DOT0 - 3 * (row - 24)
        marks = jnp.where(row < 24, marks, jnp.where((at >= 0) & (at < 3) & (row < 24 + HL), -1.0, 0.0)).astype(BF)
        for i, (own, sides) in enumerate(parts):
            frame, far_row = far_place(i, group, (m, 128), 0)
            ones = jnp.where((lane == FR0 + frame) | (lane == RW0 + far_row), 1.0, 0.0)
            side = jnp.where(lane < 32, seen(own, sides, group, 2 * HL).astype(F32), ones).astype(BF)
            shifts[group, i] = nt(marks, side)
    for h in range(HL):
        ready(h)
        for group in range(0, ZH, SPAN):
            here = slice(ZL * group, ZL * (group + SPAN))
            k = kv[here, 2 * h].reshape(n, HD)
            v = kv[here, 2 * h + 1].reshape(n, HD)
            dk = jnp.zeros((n, HD), F32)
            dv = jnp.zeros((n, HD), F32)
            for i, (own, sides) in enumerate(parts):
                q, g = seen(own, sides, group, 2 * h), seen(own, sides, group, 2 * h + 1)
                s = nt(k, q) + by_class(shifts[group, i][8 * h : 8 * h + 8])
                d = nt(v, g) + shifts[group, i][24 + h : 25 + h]
                prob = jnp.exp2(s * (SCALE * LOG2E))
                dv = dv + jnp.dot(prob.astype(BF), g, preferred_element_type=F32)
                dk = dk + jnp.dot((prob * d).astype(BF), q, preferred_element_type=F32)
            out_ref[here, 2 * h] = (dk * SCALE).astype(BF).reshape(SPAN * ZL, F, R, CH, HD)
            out_ref[here, 2 * h + 1] = dv.astype(BF).reshape(SPAN * ZL, F, R, CH, HD)


def query_grads(*refs):
    in_refs, out_refs, all_ref, bufs, sems = refs[:7], refs[7 : 7 + Z], refs[7 + Z], refs[8 + Z : 15 + Z], refs[15 + Z]
    ready = fetch(in_refs, bufs, sems)
    parts, qg = list(zip(bufs[:3], bufs[3:6])), bufs[6]
    n, m = SPAN * ZL * N, (SPAN + 2) * ZL * N
    lane = lanes(n, 128)
    masks = {}
    for group in range(0, ZH, SPAN):
        row = lax.broadcasted_iota(jnp.int32, (8, m), 0)
        for i in range(3):
            frame, far_row = far_place(i, group, (8, m), 1)
            bad = bad_frames(frame, 2 + F * group + row // R) | bad_rows(far_row, 2 + row % R)
            masks[group, i] = jnp.where(bad, BIG, 0.0)
    ready(HL)
    for h in range(HL):
        ready(h)
        for group in range(0, ZH, SPAN):
            here = slice(ZL * group, ZL * (group + SPAN))
            q = qg[here, 2 * h].reshape(n, HD)
            g = qg[here, 2 * h + 1].reshape(n, HD)
            data = qg[here, 2 * HL].astype(F32).reshape(n, 128)
            pick = lambda start: jnp.where((lane >= start) & (lane < start + 3), data, 0.0)
            lse = jnp.sum(pick(LSE0 + 3 * h), axis=-1, keepdims=True)
            dot = jnp.sum(pick(DOT0 + 3 * h), axis=-1, keepdims=True)
            dq = jnp.zeros((n, HD), F32)
            for i, (own, sides) in enumerate(parts):
                k, v = seen(own, sides, group, 2 * h), seen(own, sides, group, 2 * h + 1)
                s = nt(q, k) - lse + by_class(masks[group, i])
                d = nt(g, v) - dot
                score = (jnp.exp2(s * (SCALE * LOG2E)) * d).astype(BF)
                dq = dq + jnp.dot(score, k, preferred_element_type=F32)
            all_ref[here, h] = (dq * SCALE).astype(BF).reshape(SPAN * ZL, F, R, CH, HD)
    for k, out_ref in enumerate(out_refs):
        out_ref[...] = all_ref[lax.rem(ring_place() + k, Z)]


def unpack_kv(in_ref, *out_refs):
    for i, out_ref in enumerate(out_refs):
        for src in range(Z):
            for h in range(HL):
                at = head_of(src, h) * HD
                out_ref[:, :, :, at : at + HD] = in_ref[src, 2 * h + i]


def unpack_q(*refs):
    out_ref = refs[-1]
    for k, in_ref in enumerate(refs[:-1]):
        src = lax.rem(ring_place() + Z - k, Z)
        for h in range(HL):
            out_ref[:, :, :, head_lanes(src, h)] = in_ref[h]


def exchange(sends):
    return lax.all_to_all(sends, RING, split_axis=0, concat_axis=0, tiled=True)


def exchange_by_steps(sends):
    got = list(sends)
    for k in FAR:
        got[k] = lax.ppermute(sends[k], RING, [(i, (i + k) % Z) for i in range(Z)])
    return got


def shift(block, dx, dr):
    places = [(x, r) for x in range(NX) for r in range(NROW)]
    flat = lambda x, r: (x % NX) * NROW + r % NROW
    return lax.ppermute(block, ("x", "row"), [(flat(x + dx, r + dr), flat(x, r)) for x, r in places])


def halo(own, lo, hi):
    rows = [shift(own, 0, -1), own, shift(own, 0, 1)]
    sides = jnp.concatenate([shift(hi, -1, 0), shift(lo, 1, 0)], axis=0)
    return rows + [shift(sides, 0, -1), sides, shift(sides, 0, 1)]


def staged(blocks, last):
    whole = [pltpu.VMEM((n, blocks, F, R, CH, HD), BF) for n in (Z, Z, Z, 2 * ZL, 2 * ZL, 2 * ZL)]
    return whole + [pltpu.VMEM((Z, last, F, R, CH, HD), BF), pltpu.SemaphoreType.DMA((HL + 1, 7))]


def body(queries, key_tokens, values, outputs, grad_out, log_sums):
    lse = jnp.pad(log_sums.reshape(HEADS // ZL, F * R * CH * ZL), ((0, 4), (0, 0)))
    q_block, kv_block, dq_block = (shape(b, F, R, CH, HD) for b in (2 * HL + 1, 2 * HL, HL))
    wide = lambda block, n: shape(n, *block.shape)
    both = shape(4 * HL + 1, F, R, CH, HD)
    sent = call(pack, (both,) * Z, 6, "pack")(queries, grad_out, outputs, key_tokens, values, lse)
    got = exchange_by_steps(sent)
    q_here, q_lo, q_hi = call(
        gather_q, (wide(q_block, Z), wide(q_block, ZL), wide(q_block, ZL)), Z, "gather_q"
    )(*got)
    q_seen = halo(q_here, q_lo, q_hi)
    kv_here, kv_lo, kv_hi = call(
        gather_kv, (wide(kv_block, Z), wide(kv_block, ZL), wide(kv_block, ZL)), Z, "gather_kv", after=q_seen[4:5]
    )(*got)
    kv_seen = halo(kv_here, kv_lo, kv_hi)
    grads_kv = call(
        key_grads,
        wide(kv_block, Z),
        7,
        "key_grads",
        flops=10**10,
        scratch=staged(2 * HL + 1, 2 * HL),
        where=pl.ANY,
        after=kv_seen[4:5],
    )(*q_seen, kv_here)
    kv_back = exchange(grads_kv)
    grads_q = call(
        query_grads,
        (dq_block,) * Z,
        7,
        "query_grads",
        flops=10**11,
        scratch=[pltpu.VMEM((Z, HL, F, R, CH, HD), BF)] + staged(2 * HL, 2 * HL + 1),
        where=pl.ANY,
    )(*kv_seen, q_here)
    q_back = exchange_by_steps(grads_q)
    whole = shape(F, R, CH, HEADS * HD)
    key_out, value_out = call(unpack_kv, (whole, whole), 1, "unpack_kv")(kv_back)
    query_out = call(unpack_q, whole, Z, "unpack_q")(*q_back)
    return query_out, key_out, value_out


def solution(mesh):
    fine = Mesh(mesh.devices.reshape(NX, ZH, NROW, ZL), ("x", "zh", "row", "zl"))
    block = P(("x", "zh"), "row", "zl", None)
    return jax.shard_map(
        body,
        mesh=fine,
        in_specs=(block,) * 5 + (P("zl", ("x", "zh"), "row", None),),
        out_specs=(block,) * 3,
        check_vma=False,
    )
```

```python
import math

import jax
import jax.numpy as jnp
from jax import lax
from jax.experimental import pallas as pl
from jax.experimental.pallas import tpu as pltpu
from jax.sharding import Mesh
from jax.sharding import PartitionSpec as P

HD = 128
HEADS = 24
F, R, CH = 2, 2, 16
ZH, ZL = 4, 2
Z = ZH * ZL
N = F * R * CH
HL = HEADS // Z
FX = F * ZH
FE = FX + 4
NX, NROW = 4, 8
RING = ("zh", "zl")
FAR = (4, 3, 5, 2, 6, 1, 7)
BIG = -float(2**30)
SCALE = 1.0 / math.sqrt(HD)
LOG2E = math.log2(math.e)
DOT0, LSE0, LSE1, FR0, RW0 = 0, 16, 80, 32, 48
VMEM = 20 * 1024 * 1024
SPAN = 2
BF, F32 = jnp.bfloat16, jnp.float32


def params(**kw):
    return pltpu.CompilerParams(vmem_limit_bytes=VMEM, **kw)


def call(kernel, outs, n_in, name, flops=0, nbytes=1 << 20, scratch=(), where=pltpu.VMEM, after=()):
    whole = pl.BlockSpec(memory_space=where)
    inner = lambda *refs: kernel(*refs[:n_in], *refs[n_in + len(after) :])
    made = pl.pallas_call(
        inner,
        out_shape=outs,
        in_specs=[whole] * n_in + [pl.BlockSpec(memory_space=pl.ANY)] * len(after),
        out_specs=jax.tree.map(lambda _: pl.BlockSpec(memory_space=pltpu.VMEM), outs),
        scratch_shapes=list(scratch),
        compiler_params=params(),
        cost_estimate=pl.CostEstimate(flops=flops, bytes_accessed=nbytes, transcendentals=0),
        name=name,
    )
    return lambda *args: made(*args, *after)


def shape(*dims, dtype=BF):
    return jax.ShapeDtypeStruct(dims, dtype)


def lanes(*dims):
    return lax.broadcasted_iota(jnp.int32, dims, len(dims) - 1)


def three(x):
    hi = x.astype(BF).astype(F32)
    mid = (x - hi).astype(BF).astype(F32)
    lo = (x - hi - mid).astype(BF).astype(F32)
    return hi, mid, lo


def head_of(dest, h):
    return (HEADS // ZL) * (dest % ZL) + HL * (dest // ZL) + h


def ring_place():
    return lax.axis_index("zh") * ZL + lax.axis_index("zl")


def head_lanes(dest, h):
    return pl.ds(pl.multiple_of(head_of(dest, h) * HD, HD), HD)


def load(in_refs, bufs, sems):
    copies = [pltpu.make_async_copy(ref, buf, sems.at[i]) for i, (ref, buf) in enumerate(zip(in_refs, bufs))]
    for copy in copies:
        copy.start()
    for copy in copies:
        copy.wait()


def pack_q(*refs):
    out_refs, bufs = refs[4 : 4 + Z], refs[4 + Z : 8 + Z]
    load(refs[:4], bufs, refs[8 + Z])
    q_ref, do_ref, o_ref, lse_ref = bufs
    log_sums = jnp.concatenate([lse_ref[:, f, r] for f in range(F) for r in range(R)], axis=1)
    log_sums = jnp.concatenate([log_sums, jnp.zeros((4, 128), F32)], axis=0)
    parts = three(log_sums * math.sqrt(HD))
    row = lax.broadcasted_iota(jnp.int32, (128, 16), 0)
    col = lax.broadcasted_iota(jnp.int32, (128, 16), 1)
    spread = jnp.zeros((128, 128), F32)
    for p, part in enumerate(parts):
        put = jnp.zeros((128, 16), F32)
        for h in range(HL):
            put = jnp.where((row % 16 == 3 * h + p) & (row < 64) & (col == (row // 16) * HL + h), 1.0, put)
        spread = spread + jnp.dot(put.astype(BF), part.astype(BF), preferred_element_type=F32)
    turned = spread.T.reshape(F * R, ZL, CH, 128)
    second = pltpu.roll(turned[:, 1].reshape(N, 128), 64, 1)
    both = turned[:, 0].reshape(N, 128) + second
    lane = lanes(N, 128)
    keep = ((lane >= LSE0) & (lane < LSE0 + 9)) | ((lane >= LSE1) & (lane < LSE1 + 9))
    for k, out_ref in enumerate(out_refs):
        dest = lax.rem(ring_place() + k, Z)
        side = jnp.zeros((N, 128), F32)
        for h in range(HL):
            at = head_lanes(dest, h)
            g = do_ref[:, :, :, at]
            out_ref[2 * h] = q_ref[:, :, :, at]
            out_ref[2 * h + 1] = g
            dot = jnp.sum((g.astype(F32) * o_ref[:, :, :, at].astype(F32)).reshape(N, HD), axis=-1, keepdims=True)
            for p, part in enumerate(three(dot)):
                side = jnp.where(lane == DOT0 + 3 * h + p, part, side)
        lse = pltpu.roll(both, lax.rem(128 + LSE0 - 16 * (dest // ZL), 128), 1)
        out_ref[2 * HL] = jnp.where(keep, lse, side).astype(BF).reshape(F, R, CH, 128)


def pack_kv(*refs):
    out_ref, bufs = refs[2], refs[3:5]
    load(refs[:2], bufs, refs[5])
    for dest in range(Z):
        for h in range(HL):
            at = slice(head_of(dest, h) * HD, head_of(dest, h) * HD + HD)
            out_ref[dest, 2 * h] = bufs[0][:, :, :, at]
            out_ref[dest, 2 * h + 1] = bufs[1][:, :, :, at]


def gather_q(*refs):
    in_refs, (out_ref, lo_ref, hi_ref) = refs[:Z], refs[Z:]
    for k, in_ref in zip((0,) + FAR, in_refs):
        out_ref[lax.rem(ring_place() + Z - k, Z)] = in_ref[...]
    mine = lax.axis_index("zl")
    lane = lanes(N, 128)
    for zh in range(ZH):
        lse = out_ref[ZL * zh + mine, 2 * HL].astype(F32).reshape(N, 128)
        for zl in range(ZL):
            dot = out_ref[ZL * zh + zl, 2 * HL].astype(F32).reshape(N, 128)
            here = lse if zl == 0 else pltpu.roll(lse, 64, 1)
            side = jnp.where(lane < 16, dot, jnp.where(lane < 32, here, 0.0))
            out_ref[ZL * zh + zl, 2 * HL] = side.astype(BF).reshape(F, R, CH, 128)
    lo_ref[...] = out_ref[:ZL]
    hi_ref[...] = out_ref[Z - ZL :]


def ends(in_ref, lo_ref, hi_ref):
    lo_ref[...] = in_ref[:ZL]
    hi_ref[...] = in_ref[Z - ZL :]


def bad_frames(e, frame):
    real = lax.axis_index("x") * FX + e - 2
    return (jnp.abs(e - frame) > 2) | (real < 0) | (real >= NX * FX)


def bad_rows(e, row):
    real = lax.axis_index("row") * R + e - 2
    return (jnp.abs(e - row) > 2) | (real < 0) | (real >= NROW * R)


def far_place(part, group, dims, axis):
    token = lax.broadcasted_iota(jnp.int32, dims, axis)
    frame = F * (group + token // (ZL * N)) + (token // (R * CH)) % F
    return frame, R * part + (token // CH) % R


def seen(own, sides, group, block):
    first, last = group - 1, group + SPAN + 1
    pieces = [own[ZL * max(first, 0) : ZL * min(last, ZH), block]]
    if first < 0:
        pieces.insert(0, sides[:ZL, block])
    if last > ZH:
        pieces.append(sides[ZL:, block])
    pieces = [piece.reshape(-1, 128) for piece in pieces]
    return pieces[0] if len(pieces) == 1 else jnp.concatenate(pieces, axis=0)


def by_class(rows):
    m = rows.shape[1]
    spread = [jnp.broadcast_to(rows[i : i + 1], (CH, m)) for i in range(SPAN * F * R)]
    order = [z * F * R + i for z in range(SPAN) for _ in range(ZL) for i in range(F * R)]
    return jnp.concatenate([spread[i] for i in order], axis=0)


def nt(a, b):
    return lax.dot_general(a, b, (((1,), (1,)), ((), ())), preferred_element_type=F32)


def key_grads(*refs):
    parts, kv, out_ref = list(zip(refs[:3], refs[3:6])), refs[6], refs[7]
    n, m = SPAN * ZL * N, (SPAN + 2) * ZL * N
    lane = lanes(m, 128)
    shifts = {}
    for group in range(0, ZH, SPAN):
        dims = (32, 128)
        row = lax.broadcasted_iota(jnp.int32, dims, 0)
        pick = lanes(*dims)
        e = pick - FR0
        bad = bad_frames(e, 2 + F * group + (row % 8) // R) & (e >= 0) & (e < FE)
        marks = jnp.where(bad, BIG, 0.0)
        e = pick - RW0
        bad = bad_rows(e, 2 + row % R) & (e >= 0) & (e < R + 4)
        marks = jnp.where(bad, BIG, marks)
        at = pick - LSE0 - 3 * (row // 8)
        marks = jnp.where((at >= 0) & (at < 3), -1.0, marks)
        at = pick - DOT0 - 3 * (row - 24)
        marks = jnp.where(row < 24, marks, jnp.where((at >= 0) & (at < 3) & (row < 24 + HL), -1.0, 0.0)).astype(BF)
        for i, (own, sides) in enumerate(parts):
            frame, far_row = far_place(i, group, (m, 128), 0)
            ones = jnp.where((lane == FR0 + frame) | (lane == RW0 + far_row), 1.0, 0.0)
            side = jnp.where(lane < 32, seen(own, sides, group, 2 * HL).astype(F32), ones).astype(BF)
            shifts[group, i] = nt(marks, side)
    for h in range(HL):
        for group in range(0, ZH, SPAN):
            here = slice(ZL * group, ZL * (group + SPAN))
            k = kv[here, 2 * h].reshape(n, HD)
            v = kv[here, 2 * h + 1].reshape(n, HD)
            dk = jnp.zeros((n, HD), F32)
            dv = jnp.zeros((n, HD), F32)
            for i, (own, sides) in enumerate(parts):
                q, g = seen(own, sides, group, 2 * h), seen(own, sides, group, 2 * h + 1)
                s = nt(k, q) + by_class(shifts[group, i][8 * h : 8 * h + 8])
                d = nt(v, g) + shifts[group, i][24 + h : 25 + h]
                prob = jnp.exp2(s * (SCALE * LOG2E))
                dv = dv + jnp.dot(prob.astype(BF), g, preferred_element_type=F32)
                dk = dk + jnp.dot((prob * d).astype(BF), q, preferred_element_type=F32)
            out_ref[here, 2 * h] = (dk * SCALE).astype(BF).reshape(SPAN * ZL, F, R, CH, HD)
            out_ref[here, 2 * h + 1] = dv.astype(BF).reshape(SPAN * ZL, F, R, CH, HD)


def query_grads(*refs):
    parts, qg, out_refs, all_ref = list(zip(refs[:3], refs[3:6])), refs[6], refs[7 : 7 + Z], refs[7 + Z]
    n, m = SPAN * ZL * N, (SPAN + 2) * ZL * N
    lane = lanes(n, 128)
    masks = {}
    for group in range(0, ZH, SPAN):
        row = lax.broadcasted_iota(jnp.int32, (8, m), 0)
        for i in range(3):
            frame, far_row = far_place(i, group, (8, m), 1)
            bad = bad_frames(frame, 2 + F * group + row // R) | bad_rows(far_row, 2 + row % R)
            masks[group, i] = jnp.where(bad, BIG, 0.0)
    for h in range(HL):
        for group in range(0, ZH, SPAN):
            here = slice(ZL * group, ZL * (group + SPAN))
            q = qg[here, 2 * h].reshape(n, HD)
            g = qg[here, 2 * h + 1].reshape(n, HD)
            data = qg[here, 2 * HL].astype(F32).reshape(n, 128)
            pick = lambda start: jnp.where((lane >= start) & (lane < start + 3), data, 0.0)
            lse = jnp.sum(pick(LSE0 + 3 * h), axis=-1, keepdims=True)
            dot = jnp.sum(pick(DOT0 + 3 * h), axis=-1, keepdims=True)
            dq = jnp.zeros((n, HD), F32)
            for i, (own, sides) in enumerate(parts):
                k, v = seen(own, sides, group, 2 * h), seen(own, sides, group, 2 * h + 1)
                s = nt(q, k) - lse + by_class(masks[group, i])
                d = nt(g, v) - dot
                score = (jnp.exp2(s * (SCALE * LOG2E)) * d).astype(BF)
                dq = dq + jnp.dot(score, k, preferred_element_type=F32)
            all_ref[here, h] = (dq * SCALE).astype(BF).reshape(SPAN * ZL, F, R, CH, HD)
    for k, out_ref in enumerate(out_refs):
        out_ref[...] = all_ref[lax.rem(ring_place() + k, Z)]


def unpack_kv(in_ref, *out_refs):
    for i, out_ref in enumerate(out_refs):
        for src in range(Z):
            for h in range(HL):
                at = head_of(src, h) * HD
                out_ref[:, :, :, at : at + HD] = in_ref[src, 2 * h + i]


def unpack_q(*refs):
    out_ref = refs[-1]
    for k, in_ref in zip((0,) + FAR, refs[:-1]):
        src = lax.rem(ring_place() + Z - k, Z)
        for h in range(HL):
            out_ref[:, :, :, head_lanes(src, h)] = in_ref[h]


def exchange(sends):
    return lax.all_to_all(sends, RING, split_axis=0, concat_axis=0, tiled=True)


def exchange_by_steps(sends):
    return [sends[0]] + [lax.ppermute(sends[k], RING, [(i, (i + k) % Z) for i in range(Z)]) for k in FAR]


def shift(block, dx, dr):
    places = [(x, r) for x in range(NX) for r in range(NROW)]
    flat = lambda x, r: (x % NX) * NROW + r % NROW
    return lax.ppermute(block, ("x", "row"), [(flat(x + dx, r + dr), flat(x, r)) for x, r in places])


def join(a_ref, b_ref, out_ref):
    out_ref[:ZL] = a_ref[...]
    out_ref[ZL:] = b_ref[...]


def halo(own, lo, hi, name, fill=None):
    rows = [shift(own, 0, -1), own, shift(own, 0, 1)]
    before, after = shift(hi, -1, 0), shift(lo, 1, 0)
    filler = (fill(),) if fill else ()
    sides = call(join, shape(2 * ZL, *own.shape[1:]), 2, name, after=filler)(before, after)
    return rows + [shift(sides, 0, -1), sides, shift(sides, 0, 1)], filler


def body(queries, key_tokens, values, outputs, grad_out, log_sums):
    q_block, kv_block, dq_block = (shape(b, F, R, CH, HD) for b in (2 * HL + 1, 2 * HL, HL))
    wide = lambda block, n: shape(n, *block.shape)
    whole = shape(F, R, CH, HEADS * HD)
    room = lambda *shapes: [pltpu.VMEM(x.shape, x.dtype) for x in shapes] + [pltpu.SemaphoreType.DMA((len(shapes),))]
    sent_q = call(pack_q, (q_block,) * Z, 4, "pack_q", scratch=room(whole, whole, whole, log_sums), where=pl.ANY)(
        queries, grad_out, outputs, log_sums
    )
    q_got = exchange_by_steps(sent_q)
    sent_kv = call(
        pack_kv, wide(kv_block, Z), 2, "pack_kv", scratch=room(whole, whole), where=pl.ANY, after=q_got[1:]
    )(key_tokens, values)
    kv_here = exchange(sent_kv)
    q_here, q_lo, q_hi = call(
        gather_q, (wide(q_block, Z), wide(q_block, ZL), wide(q_block, ZL)), Z, "gather_q"
    )(*q_got)
    q_seen, _ = halo(q_here, q_lo, q_hi, "join_q")
    kv_lo, kv_hi = call(
        ends, (wide(kv_block, ZL),) * 2, 1, "ends", after=(q_seen[0], q_seen[2], q_seen[3], q_seen[5])
    )(kv_here)
    keys = lambda: call(key_grads, wide(kv_block, Z), 7, "key_grads", flops=10**10)(*q_seen, kv_here)
    kv_seen, (grads_kv,) = halo(kv_here, kv_lo, kv_hi, "join_kv", keys)
    kv_back = exchange(grads_kv)
    grads_q = call(
        query_grads,
        (dq_block,) * Z,
        7,
        "query_grads",
        flops=10**11,
        scratch=[pltpu.VMEM((Z, HL, F, R, CH, HD), BF)],
    )(*kv_seen, q_here)
    q_back = exchange_by_steps(grads_q)
    key_out, value_out = call(unpack_kv, (whole, whole), 1, "unpack_kv")(kv_back)
    query_out = call(unpack_q, whole, Z, "unpack_q")(*q_back)
    return query_out, key_out, value_out


def solution(mesh):
    fine = Mesh(mesh.devices.reshape(NX, ZH, NROW, ZL), ("x", "zh", "row", "zl"))
    block = P(("x", "zh"), "row", "zl", None)
    return jax.shard_map(
        body,
        mesh=fine,
        in_specs=(block,) * 5 + (P("zl", ("x", "zh"), "row", None),),
        out_specs=(block,) * 3,
        check_vma=False,
    )
```

```python
import math

import jax
import jax.numpy as jnp
from jax import lax
from jax.experimental import pallas as pl
from jax.experimental.pallas import tpu as pltpu
from jax.sharding import Mesh
from jax.sharding import PartitionSpec as P

HD = 128
HEADS = 24
F, R, CH = 2, 2, 16
ZH, ZL = 4, 2
Z = ZH * ZL
N = F * R * CH
HL = HEADS // Z
FX = F * ZH
FE = FX + 4
NX, NROW = 4, 8
RING = ("zh", "zl")
FAR = (4, 3, 5, 2, 6, 1, 7)
NEAR = (1, 2, 3, 4, 5, 6, 7)
BIG = -float(2**30)
SCALE = 1.0 / math.sqrt(HD)
LOG2E = math.log2(math.e)
DOT0, LSE0, LSE1, FR0, RW0 = 0, 16, 80, 32, 48
VMEM = 20 * 1024 * 1024
SPAN = 2
BF, F32 = jnp.bfloat16, jnp.float32


def call(kernel, outs, n_in, name, flops=0, nbytes=1 << 20, scratch=(), where=pltpu.VMEM, after=(), limit=VMEM, **more):
    whole = pl.BlockSpec(memory_space=where)
    inner = lambda *refs: kernel(*refs[:n_in], *refs[n_in + len(after) :])
    made = pl.pallas_call(
        inner,
        out_shape=outs,
        in_specs=[whole] * n_in + [pl.BlockSpec(memory_space=pl.ANY)] * len(after),
        out_specs=jax.tree.map(lambda _: pl.BlockSpec(memory_space=pltpu.VMEM), outs),
        scratch_shapes=list(scratch),
        compiler_params=pltpu.CompilerParams(vmem_limit_bytes=limit),
        cost_estimate=pl.CostEstimate(flops=flops, bytes_accessed=nbytes, transcendentals=0),
        name=name,
        **more,
    )
    return lambda *args: made(*args, *after)


def shape(*dims, dtype=BF):
    return jax.ShapeDtypeStruct(dims, dtype)


def lanes(*dims):
    return lax.broadcasted_iota(jnp.int32, dims, len(dims) - 1)


def three(x):
    hi = x.astype(BF).astype(F32)
    mid = (x - hi).astype(BF).astype(F32)
    lo = (x - hi - mid).astype(BF).astype(F32)
    return hi, mid, lo


def head_of(dest, h):
    return (HEADS // ZL) * (dest % ZL) + HL * (dest // ZL) + h


def ring_place():
    return lax.axis_index("zh") * ZL + lax.axis_index("zl")


def head_lanes(dest, h):
    return pl.ds(pl.multiple_of(head_of(dest, h) * HD, HD), HD)


def load(in_refs, bufs, sems):
    copies = [pltpu.make_async_copy(ref, buf, sems.at[i]) for i, (ref, buf) in enumerate(zip(in_refs, bufs))]
    for copy in copies:
        copy.start()
    for copy in copies:
        copy.wait()


def pack_q(*refs):
    out_refs, bufs = refs[4 : 4 + Z], refs[4 + Z : 8 + Z]
    load(refs[:4], bufs, refs[8 + Z])
    q_ref, do_ref, o_ref, lse_ref = bufs
    log_sums = jnp.concatenate([lse_ref[:, f, r] for f in range(F) for r in range(R)], axis=1)
    log_sums = jnp.concatenate([log_sums, jnp.zeros((4, 128), F32)], axis=0)
    parts = three(log_sums * math.sqrt(HD))
    row = lax.broadcasted_iota(jnp.int32, (128, 16), 0)
    col = lax.broadcasted_iota(jnp.int32, (128, 16), 1)
    spread = jnp.zeros((128, 128), F32)
    for p, part in enumerate(parts):
        put = jnp.zeros((128, 16), F32)
        for h in range(HL):
            put = jnp.where((row % 16 == 3 * h + p) & (row < 64) & (col == (row // 16) * HL + h), 1.0, put)
        spread = spread + jnp.dot(put.astype(BF), part.astype(BF), preferred_element_type=F32)
    turned = spread.T.reshape(F * R, ZL, CH, 128)
    second = pltpu.roll(turned[:, 1].reshape(N, 128), 64, 1)
    both = turned[:, 0].reshape(N, 128) + second
    lane = lanes(N, 128)
    keep = ((lane >= LSE0) & (lane < LSE0 + 9)) | ((lane >= LSE1) & (lane < LSE1 + 9))
    for k, out_ref in enumerate(out_refs):
        dest = lax.rem(ring_place() + k, Z)
        side = jnp.zeros((N, 128), F32)
        for h in range(HL):
            at = head_lanes(dest, h)
            g = do_ref[:, :, :, at]
            out_ref[2 * h] = q_ref[:, :, :, at]
            out_ref[2 * h + 1] = g
            dot = jnp.sum((g.astype(F32) * o_ref[:, :, :, at].astype(F32)).reshape(N, HD), axis=-1, keepdims=True)
            for p, part in enumerate(three(dot)):
                side = jnp.where(lane == DOT0 + 3 * h + p, part, side)
        lse = pltpu.roll(both, lax.rem(128 + LSE0 - 16 * (dest // ZL), 128), 1)
        out_ref[2 * HL] = jnp.where(keep, lse, side).astype(BF).reshape(F, R, CH, 128)


def pack_kv(*refs):
    out_ref, bufs = refs[2], refs[3:5]
    load(refs[:2], bufs, refs[5])
    for dest in range(Z):
        for h in range(HL):
            at = slice(head_of(dest, h) * HD, head_of(dest, h) * HD + HD)
            out_ref[dest, 2 * h] = bufs[0][:, :, :, at]
            out_ref[dest, 2 * h + 1] = bufs[1][:, :, :, at]


def gather_q(*refs):
    in_refs, (out_ref, lo_ref, hi_ref) = refs[:Z], refs[Z:]
    for k, in_ref in zip((0,) + FAR, in_refs):
        out_ref[lax.rem(ring_place() + Z - k, Z)] = in_ref[...]
    mine = lax.axis_index("zl")
    lane = lanes(N, 128)
    for zh in range(ZH):
        lse = out_ref[ZL * zh + mine, 2 * HL].astype(F32).reshape(N, 128)
        for zl in range(ZL):
            dot = out_ref[ZL * zh + zl, 2 * HL].astype(F32).reshape(N, 128)
            here = lse if zl == 0 else pltpu.roll(lse, 64, 1)
            side = jnp.where(lane < 16, dot, jnp.where(lane < 32, here, 0.0))
            out_ref[ZL * zh + zl, 2 * HL] = side.astype(BF).reshape(F, R, CH, 128)
    lo_ref[...] = out_ref[:ZL]
    hi_ref[...] = out_ref[Z - ZL :]


def ends(in_ref, lo_ref, hi_ref):
    lo_ref[...] = in_ref[:ZL]
    hi_ref[...] = in_ref[Z - ZL :]


def bad_frames(e, frame):
    real = lax.axis_index("x") * FX + e - 2
    return (jnp.abs(e - frame) > 2) | (real < 0) | (real >= NX * FX)


def bad_rows(e, row):
    real = lax.axis_index("row") * R + e - 2
    return (jnp.abs(e - row) > 2) | (real < 0) | (real >= NROW * R)


def far_place(part, group, dims, axis):
    token = lax.broadcasted_iota(jnp.int32, dims, axis)
    frame = F * (group + token // (ZL * N)) + (token // (R * CH)) % F
    return frame, R * part + (token // CH) % R


def seen(own, sides, group, block):
    first, last = group - 1, group + SPAN + 1
    pieces = [own[ZL * max(first, 0) : ZL * min(last, ZH), block]]
    if first < 0:
        pieces.insert(0, sides[:ZL, block])
    if last > ZH:
        pieces.append(sides[ZL:, block])
    pieces = [piece.reshape(-1, 128) for piece in pieces]
    return pieces[0] if len(pieces) == 1 else jnp.concatenate(pieces, axis=0)


def by_class(rows):
    m = rows.shape[1]
    spread = [jnp.broadcast_to(rows[i : i + 1], (CH, m)) for i in range(SPAN * F * R)]
    order = [z * F * R + i for z in range(SPAN) for _ in range(ZL) for i in range(F * R)]
    return jnp.concatenate([spread[i] for i in order], axis=0)


def nt(a, b):
    return lax.dot_general(a, b, (((1,), (1,)), ((), ())), preferred_element_type=F32)


def key_grads(*refs):
    parts, kv, out_ref = list(zip(refs[:3], refs[3:6])), refs[6], refs[7]
    n, m = SPAN * ZL * N, (SPAN + 2) * ZL * N
    lane = lanes(m, 128)
    shifts = {}
    for group in range(0, ZH, SPAN):
        dims = (32, 128)
        row = lax.broadcasted_iota(jnp.int32, dims, 0)
        pick = lanes(*dims)
        e = pick - FR0
        bad = bad_frames(e, 2 + F * group + (row % 8) // R) & (e >= 0) & (e < FE)
        marks = jnp.where(bad, BIG, 0.0)
        e = pick - RW0
        bad = bad_rows(e, 2 + row % R) & (e >= 0) & (e < R + 4)
        marks = jnp.where(bad, BIG, marks)
        at = pick - LSE0 - 3 * (row // 8)
        marks = jnp.where((at >= 0) & (at < 3), -1.0, marks)
        at = pick - DOT0 - 3 * (row - 24)
        marks = jnp.where(row < 24, marks, jnp.where((at >= 0) & (at < 3) & (row < 24 + HL), -1.0, 0.0)).astype(BF)
        for i, (own, sides) in enumerate(parts):
            frame, far_row = far_place(i, group, (m, 128), 0)
            ones = jnp.where((lane == FR0 + frame) | (lane == RW0 + far_row), 1.0, 0.0)
            side = jnp.where(lane < 32, seen(own, sides, group, 2 * HL).astype(F32), ones).astype(BF)
            shifts[group, i] = nt(marks, side)
    for h in range(HL):
        for group in range(0, ZH, SPAN):
            here = slice(ZL * group, ZL * (group + SPAN))
            k = kv[here, 2 * h].reshape(n, HD)
            v = kv[here, 2 * h + 1].reshape(n, HD)
            dk = jnp.zeros((n, HD), F32)
            dv = jnp.zeros((n, HD), F32)
            for i, (own, sides) in enumerate(parts):
                q, g = seen(own, sides, group, 2 * h), seen(own, sides, group, 2 * h + 1)
                s = nt(k, q) + by_class(shifts[group, i][8 * h : 8 * h + 8])
                d = nt(v, g) + shifts[group, i][24 + h : 25 + h]
                prob = jnp.exp2(s * (SCALE * LOG2E))
                dv = dv + jnp.dot(prob.astype(BF), g, preferred_element_type=F32)
                dk = dk + jnp.dot((prob * d).astype(BF), q, preferred_element_type=F32)
            out_ref[here, 2 * h] = (dk * SCALE).astype(BF).reshape(SPAN * ZL, F, R, CH, HD)
            out_ref[here, 2 * h + 1] = dv.astype(BF).reshape(SPAN * ZL, F, R, CH, HD)


def query_grads(*refs):
    parts, qg, out_refs, all_ref = list(zip(refs[:3], refs[3:6])), refs[6], refs[7 : 7 + Z], refs[7 + Z]
    n, m = SPAN * ZL * N, (SPAN + 2) * ZL * N
    lane = lanes(n, 128)
    masks = {}
    for group in range(0, ZH, SPAN):
        row = lax.broadcasted_iota(jnp.int32, (8, m), 0)
        for i in range(3):
            frame, far_row = far_place(i, group, (8, m), 1)
            bad = bad_frames(frame, 2 + F * group + row // R) | bad_rows(far_row, 2 + row % R)
            masks[group, i] = jnp.where(bad, BIG, 0.0)
    for h in range(HL):
        for group in range(0, ZH, SPAN):
            here = slice(ZL * group, ZL * (group + SPAN))
            q = qg[here, 2 * h].reshape(n, HD)
            g = qg[here, 2 * h + 1].reshape(n, HD)
            data = qg[here, 2 * HL].astype(F32).reshape(n, 128)
            pick = lambda start: jnp.where((lane >= start) & (lane < start + 3), data, 0.0)
            lse = jnp.sum(pick(LSE0 + 3 * h), axis=-1, keepdims=True)
            dot = jnp.sum(pick(DOT0 + 3 * h), axis=-1, keepdims=True)
            dq = jnp.zeros((n, HD), F32)
            for i, (own, sides) in enumerate(parts):
                k, v = seen(own, sides, group, 2 * h), seen(own, sides, group, 2 * h + 1)
                s = nt(q, k) - lse + by_class(masks[group, i])
                d = nt(g, v) - dot
                score = (jnp.exp2(s * (SCALE * LOG2E)) * d).astype(BF)
                dq = dq + jnp.dot(score, k, preferred_element_type=F32)
            all_ref[here, h] = (dq * SCALE).astype(BF).reshape(SPAN * ZL, F, R, CH, HD)
    for k, out_ref in enumerate(out_refs):
        out_ref[...] = all_ref[lax.rem(ring_place() + k, Z)]


def unpack_kv(in_ref, *out_refs):
    for i, out_ref in enumerate(out_refs):
        for src in range(Z):
            for h in range(HL):
                at = head_of(src, h) * HD
                out_ref[:, :, :, at : at + HD] = in_ref[src, 2 * h + i]


def unpack_q(*refs):
    out_ref = refs[-1]
    for k, in_ref in zip((0,) + NEAR, refs[:-1]):
        src = lax.rem(ring_place() + Z - k, Z)
        for h in range(HL):
            out_ref[:, :, :, head_lanes(src, h)] = in_ref[h]


def exchange(sends):
    return lax.all_to_all(sends, RING, split_axis=0, concat_axis=0, tiled=True)


def exchange_by_steps(sends, order):
    return [sends[0]] + [lax.ppermute(sends[k], RING, [(i, (i + k) % Z) for i in range(Z)]) for k in order]


def shift(block, dx, dr):
    places = [(x, r) for x in range(NX) for r in range(NROW)]
    flat = lambda x, r: (x % NX) * NROW + r % NROW
    return lax.ppermute(block, ("x", "row"), [(flat(x + dx, r + dr), flat(x, r)) for x, r in places])


def join(a_ref, b_ref, out_ref):
    out_ref[:ZL] = a_ref[...]
    out_ref[ZL:] = b_ref[...]


def halo(own, lo, hi, name, fill=None):
    rows = [shift(own, 0, -1), own, shift(own, 0, 1)]
    before, after = shift(hi, -1, 0), shift(lo, 1, 0)
    filler = (fill(),) if fill else ()
    sides = call(join, shape(2 * ZL, *own.shape[1:]), 2, name, after=filler)(before, after)
    return rows + [shift(sides, 0, -1), sides, shift(sides, 0, 1)], filler


def body(queries, key_tokens, values, outputs, grad_out, log_sums):
    q_block, kv_block, dq_block = (shape(b, F, R, CH, HD) for b in (2 * HL + 1, 2 * HL, HL))
    wide = lambda block, n: shape(n, *block.shape)
    whole = shape(F, R, CH, HEADS * HD)
    room = lambda *shapes: [pltpu.VMEM(x.shape, x.dtype) for x in shapes] + [pltpu.SemaphoreType.DMA((len(shapes),))]
    sent_q = call(pack_q, (q_block,) * Z, 4, "pack_q", scratch=room(whole, whole, whole, log_sums), where=pl.ANY, limit=60 * 1024 * 1024)(
        queries, grad_out, outputs, log_sums
    )
    q_got = exchange_by_steps(sent_q, FAR)
    sent_kv = call(
        pack_kv, wide(kv_block, Z), 2, "pack_kv", scratch=room(whole, whole), where=pl.ANY, after=q_got[1:]
    )(key_tokens, values)
    kv_here = exchange(sent_kv)
    q_here, q_lo, q_hi = call(
        gather_q, (wide(q_block, Z), wide(q_block, ZL), wide(q_block, ZL)), Z, "gather_q"
    )(*q_got)
    q_seen, _ = halo(q_here, q_lo, q_hi, "join_q")
    kv_lo, kv_hi = call(
        ends, (wide(kv_block, ZL),) * 2, 1, "ends", after=(q_seen[0], q_seen[2], q_seen[3], q_seen[5])
    )(kv_here)
    keys = lambda: call(key_grads, wide(kv_block, Z), 7, "key_grads", flops=10**10)(*q_seen, kv_here)
    kv_seen, (grads_kv,) = halo(kv_here, kv_lo, kv_hi, "join_kv", keys)
    kv_back = exchange(grads_kv)
    grads_q = call(
        query_grads,
        (dq_block,) * Z,
        7,
        "query_grads",
        flops=10**11,
        scratch=[pltpu.VMEM((Z, HL, F, R, CH, HD), BF)],
    )(*kv_seen, q_here)
    q_back = exchange_by_steps(grads_q, NEAR)
    key_out, value_out = call(unpack_kv, (whole, whole), 1, "unpack_kv")(kv_back)
    query_out = call(unpack_q, whole, Z, "unpack_q", after=(key_out,))(*q_back)
    return query_out, key_out, value_out


def solution(mesh):
    fine = Mesh(mesh.devices.reshape(NX, ZH, NROW, ZL), ("x", "zh", "row", "zl"))
    block = P(("x", "zh"), "row", "zl", None)
    return jax.shard_map(
        body,
        mesh=fine,
        in_specs=(block,) * 5 + (P("zl", ("x", "zh"), "row", None),),
        out_specs=(block,) * 3,
        check_vma=False,
    )
```

```python
import math

import jax
import jax.numpy as jnp
from jax import lax
from jax.experimental import pallas as pl
from jax.experimental.pallas import tpu as pltpu
from jax.sharding import Mesh
from jax.sharding import PartitionSpec as P

HD = 128
HEADS = 24
F, R, CH = 2, 2, 16
ZH, ZL = 4, 2
Z = ZH * ZL
N = F * R * CH
HL = HEADS // Z
FX = F * ZH
FE = FX + 4
NX, NROW = 4, 8
RING = ("zh", "zl")
FAR = (4, 3, 5, 2, 6, 1, 7)
NEAR = (1, 2, 3, 4, 5, 6, 7)
BIG = -float(2**30)
SCALE = 1.0 / math.sqrt(HD)
LOG2E = math.log2(math.e)
DOT0, LSE0, FR0, RW0 = 0, 16, 32, 48
VMEM = 20 * 1024 * 1024
SPAN = 2
BF, F32 = jnp.bfloat16, jnp.float32


def call(kernel, outs, n_in, name, flops=0, nbytes=1 << 20, scratch=(), where=pltpu.VMEM, after=(), limit=VMEM, **more):
    whole = pl.BlockSpec(memory_space=where)
    inner = lambda *refs: kernel(*refs[:n_in], *refs[n_in + len(after) :])
    made = pl.pallas_call(
        inner,
        out_shape=outs,
        in_specs=[whole] * n_in + [pl.BlockSpec(memory_space=pl.ANY)] * len(after),
        out_specs=jax.tree.map(lambda _: pl.BlockSpec(memory_space=pltpu.VMEM), outs),
        scratch_shapes=list(scratch),
        compiler_params=pltpu.CompilerParams(vmem_limit_bytes=limit),
        cost_estimate=pl.CostEstimate(flops=flops, bytes_accessed=nbytes, transcendentals=0),
        name=name,
        **more,
    )
    return lambda *args: made(*args, *after)


def shape(*dims, dtype=BF):
    return jax.ShapeDtypeStruct(dims, dtype)


def lanes(*dims):
    return lax.broadcasted_iota(jnp.int32, dims, len(dims) - 1)


def three(x):
    hi = x.astype(BF).astype(F32)
    mid = (x - hi).astype(BF).astype(F32)
    lo = (x - hi - mid).astype(BF).astype(F32)
    return hi, mid, lo


def head_of(dest, h):
    return (HEADS // ZL) * (dest % ZL) + HL * (dest // ZL) + h


def ring_place():
    return lax.axis_index("zh") * ZL + lax.axis_index("zl")


def head_lanes(dest, h):
    return pl.ds(pl.multiple_of(head_of(dest, h) * HD, HD), HD)


def load(in_refs, bufs, sems):
    copies = [pltpu.make_async_copy(ref, buf, sems.at[i]) for i, (ref, buf) in enumerate(zip(in_refs, bufs))]
    for copy in copies:
        copy.start()
    for copy in copies:
        copy.wait()


def pack_q(*refs):
    out_refs, bufs = refs[4 : 4 + Z], refs[4 + Z : 8 + Z]
    load(refs[:4], bufs, refs[8 + Z])
    q_ref, do_ref, o_ref, lse_ref = bufs
    log_sums = jnp.concatenate([lse_ref[:, f, r] for f in range(F) for r in range(R)], axis=1)
    log_sums = jnp.concatenate([log_sums, jnp.zeros((4, 128), F32)], axis=0)
    parts = three(log_sums * math.sqrt(HD))
    row = lax.broadcasted_iota(jnp.int32, (128, 16), 0)
    col = lax.broadcasted_iota(jnp.int32, (128, 16), 1)
    spread = jnp.zeros((128, 128), F32)
    for p, part in enumerate(parts):
        put = jnp.zeros((128, 16), F32)
        for h in range(HL):
            put = jnp.where((row % 16 == 3 * h + p) & (row < 64) & (col == (row // 16) * HL + h), 1.0, put)
        spread = spread + jnp.dot(put.astype(BF), part.astype(BF), preferred_element_type=F32)
    turned = spread.T.reshape(F * R, ZL, CH, 128)
    second = pltpu.roll(turned[:, 1].reshape(N, 128), 64, 1)
    both = turned[:, 0].reshape(N, 128) + second
    lane = lanes(N, 128)
    for k, out_ref in enumerate(out_refs):
        dest = lax.rem(ring_place() + k, Z)
        side = jnp.zeros((N, 128), F32)
        for h in range(HL):
            at = head_lanes(dest, h)
            g = do_ref[:, :, :, at]
            out_ref[8 * h : 8 * h + 4] = q_ref[:, :, :, at].reshape(4, CH, HD)
            out_ref[8 * h + 4 : 8 * h + 8] = g.reshape(4, CH, HD)
            dot = jnp.sum((g.astype(F32) * o_ref[:, :, :, at].astype(F32)).reshape(N, HD), axis=-1, keepdims=True)
            for p, part in enumerate(three(dot)):
                side = jnp.where(lane == DOT0 + 3 * h + p, part, side)
        lse = pltpu.roll(both, lax.rem(128 + 9 - 16 * (dest // ZL), 128), 1)
        side = jnp.where((lane >= 9) & (lane < 18), lse, side)
        side = jnp.where((lane >= 18) & (lane < 27), pltpu.roll(lse, 128 - 55, 1), side).reshape(F * R, CH, 128)
        packed = side[0]
        for j in range(1, F * R):
            packed = packed + pltpu.roll(side[j], 32 * j, 1)
        out_ref[8 * HL] = packed.astype(BF)


def pack_kv(*refs):
    out_ref, bufs = refs[2], refs[3:5]
    load(refs[:2], bufs, refs[5])
    for dest in range(Z):
        for h in range(HL):
            at = slice(head_of(dest, h) * HD, head_of(dest, h) * HD + HD)
            out_ref[dest, 2 * h] = bufs[0][:, :, :, at]
            out_ref[dest, 2 * h + 1] = bufs[1][:, :, :, at]


def gather_q(*refs):
    in_refs, (out_ref, lo_ref, hi_ref) = refs[:Z], refs[Z:]
    for k, in_ref in zip((0,) + FAR, in_refs):
        src = lax.rem(ring_place() + Z - k, Z)
        out_ref[src, : 2 * HL] = in_ref[: 8 * HL].reshape(2 * HL, F, R, CH, 128)
        packed = in_ref[8 * HL].astype(F32)
        for j in range(F * R):
            tile = packed if j == 0 else pltpu.roll(packed, 128 - 32 * j, 1)
            out_ref[src, 2 * HL, j // R, j % R] = tile.astype(BF)
    mine = lax.axis_index("zl")
    lane = lanes(N, 128)
    for zh in range(ZH):
        lse = out_ref[ZL * zh + mine, 2 * HL].astype(F32).reshape(N, 128)
        dots = [out_ref[ZL * zh + zl, 2 * HL].astype(F32).reshape(N, 128) for zl in range(ZL)]
        for zl, dot in enumerate(dots):
            here = pltpu.roll(lse, 7 if zl == 0 else 126, 1)
            side = jnp.where(lane < 9, dot, jnp.where((lane >= 16) & (lane < 25), here, 0.0))
            out_ref[ZL * zh + zl, 2 * HL] = side.astype(BF).reshape(F, R, CH, 128)
    lo_ref[...] = out_ref[:ZL]
    hi_ref[...] = out_ref[Z - ZL :]


def ends(in_ref, lo_ref, hi_ref):
    lo_ref[...] = in_ref[:ZL]
    hi_ref[...] = in_ref[Z - ZL :]


def bad_frames(e, frame):
    real = lax.axis_index("x") * FX + e - 2
    return (jnp.abs(e - frame) > 2) | (real < 0) | (real >= NX * FX)


def bad_rows(e, row):
    real = lax.axis_index("row") * R + e - 2
    return (jnp.abs(e - row) > 2) | (real < 0) | (real >= NROW * R)


def far_place(part, group, dims, axis):
    token = lax.broadcasted_iota(jnp.int32, dims, axis)
    frame = F * (group + token // (ZL * N)) + (token // (R * CH)) % F
    return frame, R * part + (token // CH) % R


def seen(own, sides, group, block):
    first, last = group - 1, group + SPAN + 1
    pieces = [own[ZL * max(first, 0) : ZL * min(last, ZH), block]]
    if first < 0:
        pieces.insert(0, sides[:ZL, block])
    if last > ZH:
        pieces.append(sides[ZL:, block])
    pieces = [piece.reshape(-1, 128) for piece in pieces]
    return pieces[0] if len(pieces) == 1 else jnp.concatenate(pieces, axis=0)


def by_class(rows):
    m = rows.shape[1]
    spread = [jnp.broadcast_to(rows[i : i + 1], (CH, m)) for i in range(SPAN * F * R)]
    order = [z * F * R + i for z in range(SPAN) for _ in range(ZL) for i in range(F * R)]
    return jnp.concatenate([spread[i] for i in order], axis=0)


def nt(a, b):
    return lax.dot_general(a, b, (((1,), (1,)), ((), ())), preferred_element_type=F32)


def key_grads(*refs):
    parts, kv, out_ref = list(zip(refs[:3], refs[3:6])), refs[6], refs[7]
    n, m = SPAN * ZL * N, (SPAN + 2) * ZL * N
    lane = lanes(m, 128)
    shifts = {}
    for group in range(0, ZH, SPAN):
        dims = (32, 128)
        row = lax.broadcasted_iota(jnp.int32, dims, 0)
        pick = lanes(*dims)
        e = pick - FR0
        bad = bad_frames(e, 2 + F * group + (row % 8) // R) & (e >= 0) & (e < FE)
        marks = jnp.where(bad, BIG, 0.0)
        e = pick - RW0
        bad = bad_rows(e, 2 + row % R) & (e >= 0) & (e < R + 4)
        marks = jnp.where(bad, BIG, marks)
        at = pick - LSE0 - 3 * (row // 8)
        marks = jnp.where((at >= 0) & (at < 3), -1.0, marks)
        at = pick - DOT0 - 3 * (row - 24)
        marks = jnp.where(row < 24, marks, jnp.where((at >= 0) & (at < 3) & (row < 24 + HL), -1.0, 0.0)).astype(BF)
        for i, (own, sides) in enumerate(parts):
            frame, far_row = far_place(i, group, (m, 128), 0)
            ones = jnp.where((lane == FR0 + frame) | (lane == RW0 + far_row), 1.0, 0.0)
            side = jnp.where(lane < 32, seen(own, sides, group, 2 * HL).astype(F32), ones).astype(BF)
            shifts[group, i] = nt(marks, side)
    for h in range(HL):
        for group in range(0, ZH, SPAN):
            here = slice(ZL * group, ZL * (group + SPAN))
            k = kv[here, 2 * h].reshape(n, HD)
            v = kv[here, 2 * h + 1].reshape(n, HD)
            dk = jnp.zeros((n, HD), F32)
            dv = jnp.zeros((n, HD), F32)
            for i, (own, sides) in enumerate(parts):
                q, g = seen(own, sides, group, 2 * h), seen(own, sides, group, 2 * h + 1)
                s = nt(k, q) + by_class(shifts[group, i][8 * h : 8 * h + 8])
                d = nt(v, g) + shifts[group, i][24 + h : 25 + h]
                prob = jnp.exp2(s * (SCALE * LOG2E))
                dv = dv + jnp.dot(prob.astype(BF), g, preferred_element_type=F32)
                dk = dk + jnp.dot((prob * d).astype(BF), q, preferred_element_type=F32)
            out_ref[here, 2 * h] = (dk * SCALE).astype(BF).reshape(SPAN * ZL, F, R, CH, HD)
            out_ref[here, 2 * h + 1] = dv.astype(BF).reshape(SPAN * ZL, F, R, CH, HD)


def query_grads(*refs):
    parts, qg, out_refs, all_ref = list(zip(refs[:3], refs[3:6])), refs[6], refs[7 : 7 + Z], refs[7 + Z]
    n, m = SPAN * ZL * N, (SPAN + 2) * ZL * N
    lane = lanes(n, 128)
    masks = {}
    for group in range(0, ZH, SPAN):
        row = lax.broadcasted_iota(jnp.int32, (8, m), 0)
        for i in range(3):
            frame, far_row = far_place(i, group, (8, m), 1)
            bad = bad_frames(frame, 2 + F * group + row // R) | bad_rows(far_row, 2 + row % R)
            masks[group, i] = jnp.where(bad, BIG, 0.0)
    for h in range(HL):
        for group in range(0, ZH, SPAN):
            here = slice(ZL * group, ZL * (group + SPAN))
            q = qg[here, 2 * h].reshape(n, HD)
            g = qg[here, 2 * h + 1].reshape(n, HD)
            data = qg[here, 2 * HL].astype(F32).reshape(n, 128)
            pick = lambda start: jnp.where((lane >= start) & (lane < start + 3), data, 0.0)
            lse = jnp.sum(pick(LSE0 + 3 * h), axis=-1, keepdims=True)
            dot = jnp.sum(pick(DOT0 + 3 * h), axis=-1, keepdims=True)
            dq = jnp.zeros((n, HD), F32)
            for i, (own, sides) in enumerate(parts):
                k, v = seen(own, sides, group, 2 * h), seen(own, sides, group, 2 * h + 1)
                s = nt(q, k) - lse + by_class(masks[group, i])
                d = nt(g, v) - dot
                score = (jnp.exp2(s * (SCALE * LOG2E)) * d).astype(BF)
                dq = dq + jnp.dot(score, k, preferred_element_type=F32)
            all_ref[here, h] = (dq * SCALE).astype(BF).reshape(SPAN * ZL, F, R, CH, HD)
    for k, out_ref in enumerate(out_refs):
        out_ref[...] = all_ref[lax.rem(ring_place() + k, Z)]


def unpack_kv(in_ref, *out_refs):
    for i, out_ref in enumerate(out_refs):
        for src in range(Z):
            for h in range(HL):
                at = head_of(src, h) * HD
                out_ref[:, :, :, at : at + HD] = in_ref[src, 2 * h + i]


def unpack_q(*refs):
    out_ref = refs[-1]
    for k, in_ref in zip((0,) + NEAR, refs[:-1]):
        src = lax.rem(ring_place() + Z - k, Z)
        for h in range(HL):
            out_ref[:, :, :, head_lanes(src, h)] = in_ref[h]


def exchange(sends):
    return lax.all_to_all(sends, RING, split_axis=0, concat_axis=0, tiled=True)


def exchange_by_steps(sends, order):
    return [sends[0]] + [lax.ppermute(sends[k], RING, [(i, (i + k) % Z) for i in range(Z)]) for k in order]


def shift(block, dx, dr):
    places = [(x, r) for x in range(NX) for r in range(NROW)]
    flat = lambda x, r: (x % NX) * NROW + r % NROW
    return lax.ppermute(block, ("x", "row"), [(flat(x + dx, r + dr), flat(x, r)) for x, r in places])


def join(a_ref, b_ref, out_ref):
    out_ref[:ZL] = a_ref[...]
    out_ref[ZL:] = b_ref[...]


def halo(own, lo, hi, name, fill=None):
    rows = [shift(own, 0, -1), own, shift(own, 0, 1)]
    before, after = shift(hi, -1, 0), shift(lo, 1, 0)
    filler = (fill(),) if fill else ()
    sides = call(join, shape(2 * ZL, *own.shape[1:]), 2, name, after=filler)(before, after)
    return rows + [shift(sides, 0, -1), sides, shift(sides, 0, 1)], filler


def body(queries, key_tokens, values, outputs, grad_out, log_sums):
    q_block, kv_block, dq_block = (shape(b, F, R, CH, HD) for b in (2 * HL + 1, 2 * HL, HL))
    wide = lambda block, n: shape(n, *block.shape)
    whole = shape(F, R, CH, HEADS * HD)
    room = lambda *shapes: [pltpu.VMEM(x.shape, x.dtype) for x in shapes] + [pltpu.SemaphoreType.DMA((len(shapes),))]
    sent_q = call(pack_q, (shape(8 * HL + 1, CH, HD),) * Z, 4, "pack_q", scratch=room(whole, whole, whole, log_sums), where=pl.ANY, limit=60 * 1024 * 1024)(
        queries, grad_out, outputs, log_sums
    )
    q_got = exchange_by_steps(sent_q, FAR)
    sent_kv = call(
        pack_kv, wide(kv_block, Z), 2, "pack_kv", scratch=room(whole, whole), where=pl.ANY, after=q_got[1:]
    )(key_tokens, values)
    kv_here = exchange(sent_kv)
    q_here, q_lo, q_hi = call(
        gather_q, (wide(q_block, Z), wide(q_block, ZL), wide(q_block, ZL)), Z, "gather_q"
    )(*q_got)
    q_seen, _ = halo(q_here, q_lo, q_hi, "join_q")
    kv_lo, kv_hi = call(
        ends, (wide(kv_block, ZL),) * 2, 1, "ends", after=(q_seen[0], q_seen[2], q_seen[3], q_seen[5])
    )(kv_here)
    keys = lambda: call(key_grads, wide(kv_block, Z), 7, "key_grads", flops=10**10)(*q_seen, kv_here)
    kv_seen, (grads_kv,) = halo(kv_here, kv_lo, kv_hi, "join_kv", keys)
    kv_back = exchange(grads_kv)
    grads_q = call(
        query_grads,
        (dq_block,) * Z,
        7,
        "query_grads",
        flops=10**11,
        scratch=[pltpu.VMEM((Z, HL, F, R, CH, HD), BF)],
    )(*kv_seen, q_here)
    q_back = exchange_by_steps(grads_q, NEAR)
    key_out, value_out = call(unpack_kv, (whole, whole), 1, "unpack_kv")(kv_back)
    query_out = call(unpack_q, whole, Z, "unpack_q", after=(key_out,))(*q_back)
    return query_out, key_out, value_out


def solution(mesh):
    fine = Mesh(mesh.devices.reshape(NX, ZH, NROW, ZL), ("x", "zh", "row", "zl"))
    block = P(("x", "zh"), "row", "zl", None)
    return jax.shard_map(
        body,
        mesh=fine,
        in_specs=(block,) * 5 + (P("zl", ("x", "zh"), "row", None),),
        out_specs=(block,) * 3,
        check_vma=False,
    )
```
